32 devices in a mesh: ctx: 8 (over y, x, core), ts: 4 (over z).
Axes of the slice: x: 2, y: 2, z: 4, core: 2. Of those that a mesh axis runs over, the one named last changes fastest.
Arguments:
- projected: bfloat16 [4096, 12288], P(('ctx', 'ts')), may hold values from -6 to 6
- doc_lengths: int32 [16], replicated, may hold values from 1 to 1024, 4096 in all
- short_taps: float32 [3, 7, 256], replicated, may hold values from -2.4 to 2.4
- medium_taps: float32 [128, 256], replicated, may hold values from -0.5 to 0.5
- decay_rates: float32 [16, 256], replicated, may hold values from 6.1035156e-05 to 0.03
- residues: float32 [16, 256], replicated, may hold values from -1.5 to 1.5
- skip_gain: float32 [4096], replicated, may hold values from -3 to 3
Outputs:
- hyena_out: bfloat16 [4096, 4096], P(('ctx', 'ts'))
The draws below stay inside these ranges and needn't reach their ends.
Inputs may be any that keep to these rules, and one draw needn't show every extreme that they name: `doc_lengths`: the lengths sum to 4096; the largest is exactly 1024.
All inputs are finite; a program needn't handle non-finite values.
Results may differ from the reference program's by a relative error of at most 0.01.
Values may be sent and summed in bfloat16 or wider, within the bound.
A program may use at most 128 MiB of HBM per device.

```python
import math
import jax
import jax.numpy as jnp
import numpy as np
from jax import lax

D = 4096
GROUP = 16
SHORT = 7
MEDIUM = 128
MODES = 16
DOCS = 16
GROUPS = 256
LENGTH = 4096
MAXDOC = 1024


def levels(own_key, shape, shards, smallest, largest):
    def one(dim, shards_of):
        steps = jax.random.uniform(jax.random.fold_in(jax.random.fold_in(own_key, 6), dim), (shards_of,), jnp.float32, smallest / len(shards), largest / len(shards))
        return jnp.repeat(jnp.exp(steps), shape[dim] // shards_of).reshape((-1,) + (1,) * (len(shape) - dim - 1))

    loudness = one(*shards[0])
    for cut in shards[1:]:
        loudness = loudness * one(*cut)
    return loudness


def profile(amount, total, limit, slope):
    loads = [(1 << 20) // math.isqrt(grade ** slope) + 1 for grade in range(2, amount + 1)]
    rest, holding = total - limit - (amount - 1), [1] * (amount - 1)
    while rest > 0:
        free = [i for i in range(amount - 1) if holding[i] < limit]
        whole, budget = sum([loads[i] for i in free]), rest
        for i in free:
            extra = min(limit - holding[i], max(1, budget * loads[i] // whole), rest)
            holding[i] = holding[i] + extra
            rest = rest - extra
    return np.array([limit] + holding)


def uneven_parts(key, amount, total, reach, skew):
    if amount == 2:
        one = jax.random.randint(key, (), max(1, total - reach), min(reach, total - 1) + 1)
        return jnp.stack([one, total - one])
    lengths = jnp.asarray(profile(amount, total, reach, skew), jnp.int32)
    twos = (amount - 1) // 2
    source_of, taker = lengths[1:1 + 2 * twos:2], lengths[2:2 + 2 * twos:2]
    room = jnp.minimum(source_of - 1, reach - taker)
    moved = jax.random.randint(jax.random.fold_in(key, 1), (twos,), 0, 1 << 20) % (room + 1)
    lengths = lengths.at[1:1 + 2 * twos:2].set(source_of - moved).at[2:2 + 2 * twos:2].set(taker + moved)
    return lengths[jax.random.permutation(jax.random.fold_in(key, 2), amount)]


def normal_values(stream_key, shape, spread, limit, pieces=(), dtype=jnp.bfloat16):
    drawn = jax.random.normal(stream_key, shape, jnp.float32) * spread
    if len(pieces) > 0:
        drawn = levels(stream_key, shape, pieces, -0.22, 0.18) * drawn
    return jnp.clip(drawn, min=-limit, max=limit).astype(dtype)


def setup_inputs(seed: int = 0) -> dict:
    keys = jax.random.split(jax.random.key(seed), 8)
    return {
        "projected": normal_values(keys[0], (LENGTH, 3 * D), 1.0, 6.0, ((0, 32),)),
        "doc_lengths": uneven_parts(keys[1], DOCS, LENGTH, MAXDOC, 2).astype(jnp.int32),
        "short_taps": normal_values(keys[2], (3, SHORT, GROUPS), 0.4, 2.4, (), jnp.float32),
        "medium_taps": normal_values(keys[3], (MEDIUM, GROUPS), MEDIUM ** -0.5, 0.5, (), jnp.float32),
        "decay_rates": jnp.clip(jnp.exp(jax.random.uniform(keys[4], (MODES, GROUPS), jnp.float32, math.log(6.103515625e-05), math.log(0.03))), 6.103515625e-05, 0.03),
        "residues": normal_values(keys[5], (MODES, GROUPS), 0.25, 1.5, (), jnp.float32),
        "skip_gain": normal_values(keys[6], (D,), 0.5, 3.0, (), jnp.float32),
    }


HIGHEST = lax.Precision.HIGHEST

def starts_for(positions, doc_lengths):
    doc_ends = jnp.cumsum(doc_lengths).astype(jnp.int32)
    doc_begins = (doc_ends - doc_lengths).astype(jnp.int32)
    inside = doc_begins[None, :] <= positions[:, None]
    return lax.optimization_barrier(jnp.max(jnp.where(inside, doc_begins[None, :], 0), axis=1)).astype(jnp.int32)

def featurize(window, positions, row_start, tap_table):
    row_count = positions.shape[0]
    summed = jnp.zeros((row_count,) + window.shape[1:], jnp.float32)
    for offset in range(SHORT):
        in_doc = positions - offset >= row_start
        shifted = window[SHORT - 1 - offset:SHORT - 1 - offset + row_count]
        summed = summed + jnp.where(in_doc[:, None, None], shifted * tap_table[:, offset][None], 0.0)
    return summed

def filter_tables(decay_rates, residues):
    scaled = residues * jnp.sqrt(-jnp.expm1(-2.0 * decay_rates))
    steps_f = jnp.arange(MEDIUM).astype(jnp.float32)
    long_table = lax.optimization_barrier(jnp.sum(scaled[None] * jnp.exp(-decay_rates[None] * steps_f[:, None, None]), axis=1))
    return (scaled, long_table)

def band_matrix(medium_taps, long_table, row_pos, col_pos, block_begin):
    distance = row_pos[:, None] - col_pos[None, :]
    in_band = (distance >= 0) & (distance < MEDIUM)
    lag_index = jnp.clip(distance, 0, MEDIUM - 1)
    same_block = (col_pos >= block_begin)[None, :, None]
    tap_values = medium_taps[lag_index] + jnp.where(same_block, long_table[lag_index], 0.0)
    return jnp.where(in_band[:, :, None], tap_values, 0.0)

def reference(projected, doc_lengths, short_taps, medium_taps, decay_rates, residues, skip_gain):
    groups = D // GROUP
    scaled, long_table = filter_tables(decay_rates, residues)
    taps_full = jnp.repeat(short_taps, GROUP, axis=2)
    local_rows = jnp.arange(MEDIUM).astype(jnp.int32)
    local_f = local_rows.astype(jnp.float32)
    decay_rows = scaled[None] * jnp.exp(-decay_rates[None] * (local_f + 1.0)[:, None, None])
    tail_power = jnp.exp(-decay_rates[None] * (MEDIUM - 1.0 - local_f)[:, None, None])
    block_decay = jnp.exp(-decay_rates * MEDIUM)
    blocks_total = LENGTH // MEDIUM

    def advance(carry, block_idx):
        raw_prev, product_prev, modal_state = carry
        block_begin = (block_idx * MEDIUM).astype(jnp.int32)
        current = lax.dynamic_slice_in_dim(projected, block_begin, MEDIUM, 0).astype(jnp.float32).reshape(MEDIUM, 3, D)
        positions = block_begin + local_rows
        row_start = starts_for(positions, doc_lengths)
        window = jnp.concatenate([raw_prev, current], axis=0)
        feature = featurize(window, positions, row_start, taps_full)
        product = (feature[:, 1] * feature[:, 2]).astype(jnp.bfloat16)
        col_pos = block_begin - MEDIUM + jnp.arange(2 * MEDIUM).astype(jnp.int32)
        matrix = band_matrix(medium_taps, long_table, positions, col_pos, block_begin)
        allowed = col_pos[None, :] >= row_start[:, None]
        matrix = jnp.where(allowed[:, :, None], matrix, 0.0)
        window_x = jnp.concatenate([product_prev, product], axis=0).astype(jnp.float32).reshape(2 * MEDIUM, groups, GROUP)
        banded = jnp.einsum('tug,ugc->tgc', matrix, window_x, precision=HIGHEST).reshape(MEDIUM, D)
        carried_part = jnp.einsum('tmg,mgc->tgc', decay_rows, modal_state.reshape(MODES, groups, GROUP), precision=HIGHEST).reshape(MEDIUM, D)
        carried_part = jnp.where((row_start < block_begin)[:, None], carried_part, 0.0)
        product_f = product.astype(jnp.float32)
        filtered = (banded + carried_part + skip_gain[None, :] * product_f).astype(jnp.bfloat16)
        output = (feature[:, 0] * filtered.astype(jnp.float32)).astype(jnp.bfloat16)
        last_start = row_start[MEDIUM - 1]
        kept_rows = jnp.where((positions >= last_start)[:, None], product_f, 0.0).reshape(MEDIUM, groups, GROUP)
        contribution = jnp.einsum('umg,ugc->mgc', tail_power, kept_rows, precision=HIGHEST).reshape(MODES, D)
        factor = jnp.where(last_start < block_begin, block_decay, 0.0)
        modal_state = jnp.repeat(factor, GROUP, axis=1) * modal_state + contribution
        return ((window[MEDIUM:], product, modal_state), output)
    initial = (jnp.zeros((SHORT - 1, 3, D), jnp.float32), jnp.zeros((MEDIUM, D), jnp.bfloat16), jnp.zeros((MODES, D), jnp.float32))
    finals, outputs = lax.scan(advance, initial, jnp.arange(blocks_total).astype(jnp.int32))
    return outputs.reshape(LENGTH, D)
```

```python
import functools

import jax
import jax.numpy as jnp
from jax import lax
from jax.experimental import pallas as pl
from jax.experimental.pallas import tpu as pltpu
from jax.sharding import PartitionSpec as P

GROUP = 16
SHORT = 7
MODES = 16
LANES = 128
PER = LANES // GROUP
TILE = 512
EDGE = 8


def row_starts(lengths, begin, rows):
    position = begin + lax.broadcasted_iota(jnp.int32, (rows, LANES), 0)
    start = jnp.zeros((rows, LANES), jnp.int32)
    doc_begin = jnp.int32(0)
    for doc in range(lengths.shape[0]):
        start = jnp.where(position >= doc_begin, doc_begin, start)
        doc_begin = doc_begin + lengths[doc]
    return start, position


def short_conv(value, edge, taps, part, valid, window, lane):
    rows = value.shape[0]
    columns = pl.ds(lane * LANES, LANES)
    window[pl.ds(0, EDGE), :] = edge[:, columns].astype(jnp.float32)
    window[pl.ds(EDGE, rows), :] = value[:, columns].astype(jnp.float32)
    total = window[pl.ds(EDGE, rows), :] * taps[part, 0:1, columns]
    for offset in range(1, SHORT):
        term = window[pl.ds(EDGE - offset, rows), :] * taps[part, offset : offset + 1, columns]
        total = total + jnp.where(valid >= offset, term, 0.0)
    return total


def on_diagonal(shape):
    row = lax.broadcasted_iota(jnp.int32, shape, 0) // GROUP
    column = lax.broadcasted_iota(jnp.int32, shape, 1) // GROUP
    return row == column


def spread(block):
    lane_group = lax.broadcasted_iota(jnp.int32, (1, LANES), 1) // GROUP
    parts = [jnp.where(lane_group == g, block, 0.0) for g in range(PER)]
    return jnp.concatenate(parts, axis=0).astype(jnp.bfloat16)


def circulants(rows_ref, lane, mask, band):
    for g in range(PER):
        taps = rows_ref[pl.ds(lane * PER + g, 1), :]
        wheel = pltpu.roll(
            jnp.broadcast_to(taps, (LANES, LANES)), 0, 1, stride=1, stride_axis=0
        )
        band[:, pl.ds(g * LANES, LANES)] = jnp.where(mask, wheel, 0.0).astype(jnp.bfloat16)


def product_kernel(lengths, begin, k_ref, v_ref, ke_ref, ve_ref, taps, tail, out, state, window):
    rows = k_ref.shape[0]
    start, position = row_starts(lengths, begin[0], rows)
    valid = position - start
    last = jnp.max(start)
    diagonal = on_diagonal((LANES, LANES))
    for lane in range(TILE // LANES):
        columns = pl.ds(lane * LANES, LANES)
        key = short_conv(k_ref, ke_ref, taps, 1, valid, window.at[0], lane)
        value = short_conv(v_ref, ve_ref, taps, 2, valid, window.at[1], lane)
        product = (key * value).astype(jnp.bfloat16)
        out[:, columns] = product
        kept = jnp.where(position >= last, product.astype(jnp.float32), 0.0).astype(jnp.bfloat16)
        full = jnp.dot(tail[columns, :], kept, preferred_element_type=jnp.float32)
        full = jnp.where(diagonal, full, 0.0)
        summed = full[0:MODES]
        for g in range(1, PER):
            summed = summed + full[g * MODES : (g + 1) * MODES]
        state[:, columns] = summed


def local_kernel(
    lengths, begin, x_ref, q_ref, qe_ref, taps, wheel, skip, partial, query, window, band
):
    rows = x_ref.shape[0]
    start, position = row_starts(lengths, begin[0], rows)
    valid = position - start
    row = lax.broadcasted_iota(jnp.int32, (rows, LANES), 0)
    column = lax.broadcasted_iota(jnp.int32, (rows, LANES), 1)
    mask = (column <= row) & (column + begin[0] >= start)
    for lane in range(TILE // LANES):
        columns = pl.ds(lane * LANES, LANES)
        query[:, columns] = short_conv(q_ref, qe_ref, taps, 0, valid, window, lane)
        block = x_ref[:, columns].astype(jnp.float32)
        circulants(wheel, lane, mask, band.at[lane % 2])
        summed = jnp.dot(band[lane % 2], spread(block), preferred_element_type=jnp.float32)
        partial[:, columns] = summed + skip[:, columns] * block


def final_kernel(
    lengths, begin, x_ref, wheel, decay, state, partial, query, out, band
):
    rows = x_ref.shape[0]
    start, position = row_starts(lengths, begin[0], rows)
    row = lax.broadcasted_iota(jnp.int32, (rows, LANES), 0)
    column = lax.broadcasted_iota(jnp.int32, (rows, LANES), 1)
    mask = (column > row) & (column + (begin[0] - rows) >= start)
    carried_rows = start < begin[0]
    diagonal = on_diagonal((LANES, LANES))
    for lane in range(TILE // LANES):
        columns = pl.ds(lane * LANES, LANES)
        block = x_ref[:, columns].astype(jnp.float32)
        circulants(wheel, lane, mask, band.at[lane % 2])
        summed = jnp.dot(band[lane % 2], spread(block), preferred_element_type=jnp.float32)
        stacked = jnp.concatenate([state[:, columns]] * PER, axis=0)
        stacked = jnp.where(diagonal, stacked, 0.0).astype(jnp.bfloat16)
        carried = jnp.dot(decay[:, columns], stacked, preferred_element_type=jnp.float32)
        carried = jnp.where(carried_rows, carried, 0.0)
        filtered = (partial[:, columns] + summed + carried).astype(jnp.bfloat16)
        out[:, columns] = (query[:, columns] * filtered.astype(jnp.float32)).astype(jnp.bfloat16)


def block(shape, index):
    return pl.BlockSpec(shape, index)


def per_device(projected, doc_lengths, short_taps, medium_taps, decay_rates, residues, skip_gain):
    ts_count, ctx_count = lax.axis_size("ts"), lax.axis_size("ctx")
    ts_index, ctx_index = lax.axis_index("ts"), lax.axis_index("ctx")
    rows, width = projected.shape[0], projected.shape[1] // 3
    total = rows * ts_count * ctx_count
    span = rows * ts_count
    reach = -(-(total // 4) // span)
    devices = ts_count * ctx_count
    pairs = [(i, i + 1) for i in range(devices - 1)]
    everyone = ("ctx", "ts")
    tiles = width // TILE
    groups_tile = TILE // GROUP

    edge_kv = lax.ppermute(projected[rows - EDGE :, width:], everyone, pairs)
    edge_q = lax.ppermute(projected[rows - EDGE :, :width], everyone, pairs)

    begin = (ctx_index * ts_count + ts_index) * rows
    begin_array = jnp.full((1,), begin, jnp.int32)
    steps = jnp.arange(rows, dtype=jnp.float32)
    back = (rows - jnp.arange(rows)) % rows
    back_f = back.astype(jnp.float32)
    scaled = residues * jnp.sqrt(-jnp.expm1(-2.0 * decay_rates))
    medium_rows = jnp.concatenate([medium_taps[:1], medium_taps[:0:-1]], axis=0).T
    long_rows = jnp.sum(
        scaled[:, :, None] * jnp.exp(-decay_rates[:, :, None] * back_f[None, None]), axis=0
    )
    own_rows = medium_rows + long_rows
    rates_flat = decay_rates.T.reshape(-1)
    scaled_flat = scaled.T.reshape(-1)
    tail = jnp.exp(-rates_flat[:, None] * (rows - 1.0 - steps)[None, :]).astype(jnp.bfloat16)
    decay = (scaled_flat[None] * jnp.exp(-rates_flat[None] * (steps + 1.0)[:, None])).astype(
        jnp.bfloat16
    )
    taps = jnp.repeat(short_taps, GROUP, axis=2)
    rates_wide = jnp.repeat(decay_rates, GROUP, axis=1)

    smem = pl.BlockSpec(memory_space=pltpu.SMEM)
    tile = lambda part=0: block((rows, TILE), lambda i: (0, i + part * tiles))
    edge = lambda part=0: block((EDGE, TILE), lambda i: (0, i + part * tiles))
    taps_tile = block((3, SHORT, TILE), lambda i: (0, 0, i))
    state_tile = block((MODES, TILE), lambda i: (0, i))
    wheel_tile = block((groups_tile, rows), lambda i: (i, 0))
    wide = lambda dtype: jax.ShapeDtypeStruct((rows, width), dtype)
    product, state = pl.pallas_call(
        product_kernel,
        grid=(tiles,),
        in_specs=[smem, smem, tile(1), tile(2), edge(0), edge(1), taps_tile,
                  block((TILE, rows), lambda i: (i, 0))],
        out_specs=[tile(), state_tile],
        out_shape=[wide(jnp.bfloat16), jax.ShapeDtypeStruct((MODES, width), jnp.float32)],
        scratch_shapes=[pltpu.VMEM((2, EDGE + rows, LANES), jnp.float32)],
        name="product",
    )(doc_lengths, begin_array, projected, projected, edge_kv, edge_kv, taps, tail)

    before = lax.ppermute(product, everyone, pairs)

    ends = jnp.cumsum(doc_lengths)
    begins = ends - doc_lengths

    def start_of(position):
        return jnp.max(jnp.where(begins <= position, begins, 0))

    def faded(distance, alive):
        return jnp.where(alive, jnp.exp(-rates_wide * (distance * jnp.float32(rows))), 0.0)

    last_own = start_of(begin + rows - 1)
    last_before = start_of(jnp.maximum(begin - 1, 0))
    span_begin = ctx_index * span
    last_span = start_of(span_begin + span - 1)
    to_end = (ts_count - 1 - ts_index).astype(jnp.float32)
    step_in = faded(1.0, last_own < begin)
    running, entered = state, jnp.zeros_like(state)
    rest = state * faded(to_end, last_span <= begin + rows - 1)
    for hop in range(ts_count - 1):
        got = lax.ppermute(running.astype(jnp.bfloat16), "ts", [(hop, hop + 1)])
        back_hop = ts_count - 1 - hop
        got_rest = lax.ppermute(rest.astype(jnp.bfloat16), "ts", [(back_hop, back_hop - 1)])
        got = got.astype(jnp.float32)
        entered = entered + got
        running = running + step_in * got
        rest = rest + got_rest.astype(jnp.float32)
    whole = rest + faded(to_end + 1.0, last_span < begin) * entered
    whole = whole.astype(jnp.bfloat16)
    for hop in range(1, reach + 1):
        if hop >= ctx_count:
            break
        got = lax.ppermute(whole, "ctx", [(i, i + hop) for i in range(ctx_count - hop)])
        distance = (ts_index + (hop - 1) * ts_count).astype(jnp.float32)
        alive = last_before <= span_begin - (hop - 1) * span - 1
        entered = entered + faded(distance, alive) * got.astype(jnp.float32)

    partial, query = pl.pallas_call(
        local_kernel,
        grid=(tiles,),
        in_specs=[smem, smem, tile(), tile(), edge(), taps_tile, wheel_tile,
                  block((1, TILE), lambda i: (0, i))],
        out_specs=[tile(), tile()],
        out_shape=[wide(jnp.float32), wide(jnp.float32)],
        scratch_shapes=[
            pltpu.VMEM((EDGE + rows, LANES), jnp.float32),
            pltpu.VMEM((2, rows, PER * LANES), jnp.bfloat16),
        ],
        cost_estimate=pl.CostEstimate(
            flops=2 * rows * rows * width * PER, bytes_accessed=rows * width * 12, transcendentals=0
        ),
        name="local",
    )(doc_lengths, begin_array, product, projected, edge_q, taps, own_rows, skip_gain[None])

    return pl.pallas_call(
        final_kernel,
        grid=(tiles,),
        in_specs=[smem, smem, tile(), wheel_tile, tile(), state_tile, tile(), tile()],
        out_specs=tile(),
        out_shape=wide(jnp.bfloat16),
        scratch_shapes=[pltpu.VMEM((2, rows, PER * LANES), jnp.bfloat16)],
        name="final",
    )(doc_lengths, begin_array, before, medium_rows, decay, entered, partial, query)


def solution(mesh):
    return jax.shard_map(
        per_device,
        mesh=mesh,
        in_specs=(P(("ctx", "ts"), None), P(), P(), P(), P(), P(), P()),
        out_specs=P(("ctx", "ts"), None),
        check_vma=False,
    )
```

```python
import functools

import jax
import jax.numpy as jnp
from jax import lax
from jax.experimental import pallas as pl
from jax.experimental.pallas import tpu as pltpu
from jax.sharding import PartitionSpec as P

GROUP = 16
SHORT = 7
MODES = 16
LANES = 128
PER = LANES // GROUP
TILE = 512
EDGE = 8


def row_starts(lengths, begin, rows):
    position = begin + lax.broadcasted_iota(jnp.int32, (rows, LANES), 0)
    start = jnp.zeros((rows, LANES), jnp.int32)
    doc_begin = jnp.int32(0)
    for doc in range(lengths.shape[0]):
        start = jnp.where(position >= doc_begin, doc_begin, start)
        doc_begin = doc_begin + lengths[doc]
    return start, position


def short_conv(value, edge, taps, part, valid, window, lane):
    rows = value.shape[0]
    columns = pl.ds(lane * LANES, LANES)
    window[pl.ds(0, EDGE), :] = edge[:, columns].astype(jnp.float32)
    window[pl.ds(EDGE, rows), :] = value[:, columns].astype(jnp.float32)
    total = window[pl.ds(EDGE, rows), :] * taps[part, 0:1, columns]
    for offset in range(1, SHORT):
        term = window[pl.ds(EDGE - offset, rows), :] * taps[part, offset : offset + 1, columns]
        total = total + jnp.where(valid >= offset, term, 0.0)
    return total


def on_diagonal(shape):
    row = lax.broadcasted_iota(jnp.int32, shape, 0) // GROUP
    column = lax.broadcasted_iota(jnp.int32, shape, 1) // GROUP
    return row == column


def spread(block):
    lane_group = lax.broadcasted_iota(jnp.int32, (1, LANES), 1) // GROUP
    parts = [jnp.where(lane_group == g, block, 0.0) for g in range(PER)]
    return jnp.concatenate(parts, axis=0).astype(jnp.bfloat16)


def circulants(rows_ref, lane, mask, band):
    for g in range(PER):
        taps = rows_ref[pl.ds(lane * PER + g, 1), :]
        wheel = pltpu.roll(
            jnp.broadcast_to(taps, (LANES, LANES)), 0, 1, stride=1, stride_axis=0
        )
        band[:, pl.ds(g * LANES, LANES)] = jnp.where(mask, wheel, 0.0).astype(jnp.bfloat16)


def product_kernel(lengths, begin, k_ref, v_ref, ke_ref, ve_ref, taps, tail, out, state, window):
    rows = k_ref.shape[0]
    start, position = row_starts(lengths, begin[0], rows)
    valid = position - start
    last = jnp.max(start)
    diagonal = on_diagonal((LANES, LANES))
    for lane in range(TILE // LANES):
        columns = pl.ds(lane * LANES, LANES)
        key = short_conv(k_ref, ke_ref, taps, 1, valid, window.at[0], lane)
        value = short_conv(v_ref, ve_ref, taps, 2, valid, window.at[1], lane)
        product = (key * value).astype(jnp.bfloat16)
        out[:, columns] = product
        kept = jnp.where(position >= last, product.astype(jnp.float32), 0.0).astype(jnp.bfloat16)
        full = jnp.dot(tail[columns, :], kept, preferred_element_type=jnp.float32)
        full = jnp.where(diagonal, full, 0.0)
        summed = full[0:MODES]
        for g in range(1, PER):
            summed = summed + full[g * MODES : (g + 1) * MODES]
        state[:, columns] = summed


def local_kernel(
    lengths, begin, x_ref, q_ref, qe_ref, taps, wheel, skip, partial, query, window, band
):
    rows = x_ref.shape[0]
    start, position = row_starts(lengths, begin[0], rows)
    valid = position - start
    row = lax.broadcasted_iota(jnp.int32, (rows, LANES), 0)
    column = lax.broadcasted_iota(jnp.int32, (rows, LANES), 1)
    mask = (column <= row) & (column + begin[0] >= start)
    for lane in range(TILE // LANES):
        columns = pl.ds(lane * LANES, LANES)
        query[:, columns] = short_conv(q_ref, qe_ref, taps, 0, valid, window, lane)
        block = x_ref[:, columns].astype(jnp.float32)
        circulants(wheel, lane, mask, band.at[lane % 2])
        summed = jnp.dot(band[lane % 2], spread(block), preferred_element_type=jnp.float32)
        partial[:, columns] = summed + skip[:, columns] * block


def final_kernel(
    lengths, begin, x_ref, wheel, decay, state, partial, query, out, band
):
    rows = x_ref.shape[0]
    start, position = row_starts(lengths, begin[0], rows)
    row = lax.broadcasted_iota(jnp.int32, (rows, LANES), 0)
    column = lax.broadcasted_iota(jnp.int32, (rows, LANES), 1)
    mask = (column > row) & (column + (begin[0] - rows) >= start)
    carried_rows = start < begin[0]
    diagonal = on_diagonal((LANES, LANES))
    for lane in range(TILE // LANES):
        columns = pl.ds(lane * LANES, LANES)
        block = x_ref[:, columns].astype(jnp.float32)
        circulants(wheel, lane, mask, band.at[lane % 2])
        summed = jnp.dot(band[lane % 2], spread(block), preferred_element_type=jnp.float32)
        stacked = jnp.concatenate([state[:, columns]] * PER, axis=0)
        stacked = jnp.where(diagonal, stacked, 0.0).astype(jnp.bfloat16)
        carried = jnp.dot(decay[:, columns], stacked, preferred_element_type=jnp.float32)
        carried = jnp.where(carried_rows, carried, 0.0)
        filtered = (partial[:, columns] + summed + carried).astype(jnp.bfloat16)
        out[:, columns] = (query[:, columns] * filtered.astype(jnp.float32)).astype(jnp.bfloat16)


def block(shape, index):
    return pl.BlockSpec(shape, index)


def per_device(projected, doc_lengths, short_taps, medium_taps, decay_rates, residues, skip_gain):
    ts_count, ctx_count = lax.axis_size("ts"), lax.axis_size("ctx")
    ts_index, ctx_index = lax.axis_index("ts"), lax.axis_index("ctx")
    rows, width = projected.shape[0], projected.shape[1] // 3
    total = rows * ts_count * ctx_count
    span = rows * ts_count
    reach = -(-(total // 4) // span)
    devices = ts_count * ctx_count
    pairs = [(i, i + 1) for i in range(devices - 1)]
    everyone = ("ctx", "ts")
    tiles = width // TILE
    groups_tile = TILE // GROUP

    edge_kv = lax.ppermute(projected[rows - EDGE :, width:], everyone, pairs)
    edge_q = lax.ppermute(projected[rows - EDGE :, :width], everyone, pairs)

    begin = (ctx_index * ts_count + ts_index) * rows
    begin_array = jnp.full((1,), begin, jnp.int32)
    steps = jnp.arange(rows, dtype=jnp.float32)
    back = (rows - jnp.arange(rows)) % rows
    back_f = back.astype(jnp.float32)
    scaled = residues * jnp.sqrt(-jnp.expm1(-2.0 * decay_rates))
    medium_rows = jnp.concatenate([medium_taps[:1], medium_taps[:0:-1]], axis=0).T
    long_rows = jnp.sum(
        scaled[:, :, None] * jnp.exp(-decay_rates[:, :, None] * back_f[None, None]), axis=0
    )
    own_rows = medium_rows + long_rows
    rates_flat = decay_rates.T.reshape(-1)
    scaled_flat = scaled.T.reshape(-1)
    tail = jnp.exp(-rates_flat[:, None] * (rows - 1.0 - steps)[None, :]).astype(jnp.bfloat16)
    decay = (scaled_flat[None] * jnp.exp(-rates_flat[None] * (steps + 1.0)[:, None])).astype(
        jnp.bfloat16
    )
    taps = jnp.repeat(short_taps, GROUP, axis=2)
    rates_wide = lax.optimization_barrier(jnp.repeat(decay_rates, GROUP, axis=1))
    ends = jnp.cumsum(doc_lengths)
    begins = ends - doc_lengths

    def start_of(position):
        return jnp.max(jnp.where(begins <= position, begins, 0))

    last_own = start_of(begin + rows - 1)
    last_before = start_of(jnp.maximum(begin - 1, 0))
    span_begin = ctx_index * span
    last_span = start_of(span_begin + span - 1)
    edge_kv, edge_q, decay, own_rows, tail, taps, rates_wide, medium_rows, last_own, last_before, last_span = (
        lax.optimization_barrier(
            (edge_kv, edge_q, decay, own_rows, tail, taps, rates_wide, medium_rows, last_own, last_before, last_span)
        )
    )

    smem = pl.BlockSpec(memory_space=pltpu.SMEM)
    tile = lambda part=0: block((rows, TILE), lambda i: (0, i + part * tiles))
    edge = lambda part=0: block((EDGE, TILE), lambda i: (0, i + part * tiles))
    taps_tile = block((3, SHORT, TILE), lambda i: (0, 0, i))
    state_tile = block((MODES, TILE), lambda i: (0, i))
    wheel_tile = block((groups_tile, rows), lambda i: (i, 0))
    wide = lambda dtype: jax.ShapeDtypeStruct((rows, width), dtype)
    product, state = pl.pallas_call(
        product_kernel,
        grid=(tiles,),
        in_specs=[smem, smem, tile(1), tile(2), edge(0), edge(1), taps_tile,
                  block((TILE, rows), lambda i: (i, 0))],
        out_specs=[tile(), state_tile],
        out_shape=[wide(jnp.bfloat16), jax.ShapeDtypeStruct((MODES, width), jnp.float32)],
        scratch_shapes=[pltpu.VMEM((2, EDGE + rows, LANES), jnp.float32)],
        name="product",
    )(doc_lengths, begin_array, projected, projected, edge_kv, edge_kv, taps, tail)

    before = lax.ppermute(product, everyone, pairs)

    partial, query = pl.pallas_call(
        local_kernel,
        grid=(tiles,),
        in_specs=[smem, smem, tile(), tile(), edge(), taps_tile, wheel_tile,
                  block((1, TILE), lambda i: (0, i))],
        out_specs=[tile(), tile()],
        out_shape=[wide(jnp.float32), wide(jnp.float32)],
        scratch_shapes=[
            pltpu.VMEM((EDGE + rows, LANES), jnp.float32),
            pltpu.VMEM((2, rows, PER * LANES), jnp.bfloat16),
        ],
        cost_estimate=pl.CostEstimate(
            flops=16 * rows * rows * width * PER, bytes_accessed=rows * width * 12, transcendentals=0
        ),
        name="local",
    )(doc_lengths, begin_array, product, projected, edge_q, taps, own_rows, skip_gain[None])

    def faded(distance, alive):
        return jnp.where(alive, jnp.exp(-rates_wide * (distance * jnp.float32(rows))), 0.0)

    to_end = (ts_count - 1 - ts_index).astype(jnp.float32)
    step_in = faded(1.0, last_own < begin)
    running, entered = state, jnp.zeros_like(state)
    rest = state * faded(to_end, last_span <= begin + rows - 1)
    for hop in range(ts_count - 1):
        got = lax.ppermute(running.astype(jnp.bfloat16), "ts", [(hop, hop + 1)])
        back_hop = ts_count - 1 - hop
        got_rest = lax.ppermute(rest.astype(jnp.bfloat16), "ts", [(back_hop, back_hop - 1)])
        got = got.astype(jnp.float32)
        entered = entered + got
        if hop == 0:
            got, got_rest, partial, query = lax.optimization_barrier(
                (got, got_rest, partial, query)
            )
        running = running + step_in * got
        rest = rest + got_rest.astype(jnp.float32)
    whole = rest + faded(to_end + 1.0, last_span < begin) * entered
    whole = whole.astype(jnp.bfloat16)
    for hop in range(1, reach + 1):
        if hop >= ctx_count:
            break
        got = lax.ppermute(whole, "ctx", [(i, i + hop) for i in range(ctx_count - hop)])
        distance = (ts_index + (hop - 1) * ts_count).astype(jnp.float32)
        alive = last_before <= span_begin - (hop - 1) * span - 1
        entered = entered + faded(distance, alive) * got.astype(jnp.float32)

    return pl.pallas_call(
        final_kernel,
        grid=(tiles,),
        in_specs=[smem, smem, tile(), wheel_tile, tile(), state_tile, tile(), tile()],
        out_specs=tile(),
        out_shape=wide(jnp.bfloat16),
        scratch_shapes=[pltpu.VMEM((2, rows, PER * LANES), jnp.bfloat16)],
        name="final",
    )(doc_lengths, begin_array, before, medium_rows, decay, entered, partial, query)


def solution(mesh):
    return jax.shard_map(
        per_device,
        mesh=mesh,
        in_specs=(P(("ctx", "ts"), None), P(), P(), P(), P(), P(), P()),
        out_specs=P(("ctx", "ts"), None),
        check_vma=False,
    )
```

```python
import functools

import jax
import jax.numpy as jnp
from jax import lax
from jax.experimental import pallas as pl
from jax.experimental.pallas import tpu as pltpu
from jax.sharding import PartitionSpec as P

GROUP = 16
SHORT = 7
MODES = 16
LANES = 128
PER = LANES // GROUP
TILE = 512
EDGE = 8


def row_starts(lengths, begin, rows):
    position = begin + lax.broadcasted_iota(jnp.int32, (rows, LANES), 0)
    start = jnp.zeros((rows, LANES), jnp.int32)
    doc_begin = jnp.int32(0)
    for doc in range(lengths.shape[0]):
        start = jnp.where(position >= doc_begin, doc_begin, start)
        doc_begin = doc_begin + lengths[doc]
    return start, position


def short_conv(value, edge, taps, part, valid, window, lane):
    rows = value.shape[0]
    columns = pl.ds(lane * LANES, LANES)
    window[pl.ds(0, EDGE), :] = edge[:, columns].astype(jnp.float32)
    window[pl.ds(EDGE, rows), :] = value[:, columns].astype(jnp.float32)
    total = window[pl.ds(EDGE, rows), :] * taps[part, 0:1, columns]
    for offset in range(1, SHORT):
        term = window[pl.ds(EDGE - offset, rows), :] * taps[part, offset : offset + 1, columns]
        total = total + jnp.where(valid >= offset, term, 0.0)
    return total


def on_diagonal(shape):
    row = lax.broadcasted_iota(jnp.int32, shape, 0) // GROUP
    column = lax.broadcasted_iota(jnp.int32, shape, 1) // GROUP
    return row == column


def spread(block):
    lane_group = lax.broadcasted_iota(jnp.int32, (1, LANES), 1) // GROUP
    parts = [jnp.where(lane_group == g, block, 0.0) for g in range(PER)]
    return jnp.concatenate(parts, axis=0).astype(jnp.bfloat16)


def circulants(rows_ref, lane, mask, band):
    for g in range(PER):
        taps = rows_ref[pl.ds(lane * PER + g, 1), :]
        wheel = pltpu.roll(
            jnp.broadcast_to(taps, (LANES, LANES)), 0, 1, stride=1, stride_axis=0
        )
        band[:, pl.ds(g * LANES, LANES)] = jnp.where(mask, wheel, 0.0).astype(jnp.bfloat16)


def product_kernel(lengths, begin, k_ref, v_ref, ke_ref, ve_ref, taps, tail, out, state, window):
    rows = k_ref.shape[0]
    start, position = row_starts(lengths, begin[0], rows)
    valid = position - start
    last = jnp.max(start)
    diagonal = on_diagonal((LANES, LANES))
    for lane in range(TILE // LANES):
        columns = pl.ds(lane * LANES, LANES)
        key = short_conv(k_ref, ke_ref, taps, 1, valid, window.at[0], lane)
        value = short_conv(v_ref, ve_ref, taps, 2, valid, window.at[1], lane)
        product = (key * value).astype(jnp.bfloat16)
        out[:, columns] = product
        kept = jnp.where(position >= last, product.astype(jnp.float32), 0.0).astype(jnp.bfloat16)
        full = jnp.dot(tail[columns, :], kept, preferred_element_type=jnp.float32)
        full = jnp.where(diagonal, full, 0.0)
        summed = full[0:MODES]
        for g in range(1, PER):
            summed = summed + full[g * MODES : (g + 1) * MODES]
        state[:, columns] = summed


def local_kernel(
    lengths, begin, x_ref, q_ref, qe_ref, taps, wheel, skip, partial, query, window, band
):
    rows = x_ref.shape[0]
    start, position = row_starts(lengths, begin[0], rows)
    valid = position - start
    row = lax.broadcasted_iota(jnp.int32, (rows, LANES), 0)
    column = lax.broadcasted_iota(jnp.int32, (rows, LANES), 1)
    mask = (column <= row) & (column + begin[0] >= start)
    for lane in range(TILE // LANES):
        columns = pl.ds(lane * LANES, LANES)
        query[:, columns] = short_conv(q_ref, qe_ref, taps, 0, valid, window, lane)
        block = x_ref[:, columns].astype(jnp.float32)
        circulants(wheel, lane, mask, band.at[lane % 2])
        summed = jnp.dot(band[lane % 2], spread(block), preferred_element_type=jnp.float32)
        partial[:, columns] = summed + skip[:, columns] * block


def final_kernel(
    lengths, begin, x_ref, wheel, decay, state, partial, query, out, band
):
    rows = x_ref.shape[0]
    start, position = row_starts(lengths, begin[0], rows)
    row = lax.broadcasted_iota(jnp.int32, (rows, LANES), 0)
    column = lax.broadcasted_iota(jnp.int32, (rows, LANES), 1)
    mask = (column > row) & (column + (begin[0] - rows) >= start)
    carried_rows = start < begin[0]
    diagonal = on_diagonal((LANES, LANES))
    for lane in range(TILE // LANES):
        columns = pl.ds(lane * LANES, LANES)
        block = x_ref[:, columns].astype(jnp.float32)
        circulants(wheel, lane, mask, band.at[lane % 2])
        summed = jnp.dot(band[lane % 2], spread(block), preferred_element_type=jnp.float32)
        stacked = jnp.concatenate([state[:, columns]] * PER, axis=0)
        stacked = jnp.where(diagonal, stacked, 0.0).astype(jnp.bfloat16)
        carried = jnp.dot(decay[:, columns], stacked, preferred_element_type=jnp.float32)
        carried = jnp.where(carried_rows, carried, 0.0)
        filtered = (partial[:, columns] + summed + carried).astype(jnp.bfloat16)
        out[:, columns] = (query[:, columns] * filtered.astype(jnp.float32)).astype(jnp.bfloat16)


def exchange_kernel(
    ctx_count, ts_count, reach, rows, flags, product, state, rates, before, entered,
    rest, run_out, run_in, rest_out, rest_in, whole_out, cross_in, send, recv
):
    ctx, ts = lax.axis_index("ctx"), lax.axis_index("ts")
    me = ctx * ts_count + ts
    has_before, has_after = me > 0, me < ctx_count * ts_count - 1
    after, ahead = me + 1, me - 1 + ctx_count * ts_count

    def place(index):
        return (lax.rem(lax.div(index, ts_count), ctx_count), lax.rem(index, ts_count))

    def copy(source, target, slot, device):
        return pltpu.make_async_remote_copy(
            src_ref=source, dst_ref=target, send_sem=send.at[slot], recv_sem=recv.at[slot],
            device_id=device, device_id_type=pl.DeviceIdType.MESH,
        )

    def faded(distance, flag):
        return jnp.exp(rates[...] * (-jnp.float32(rows) * distance)) * flags[flag]

    barrier = pltpu.get_barrier_semaphore()

    def greet(device):
        pl.semaphore_signal(
            barrier, inc=1, device_id=device, device_id_type=pl.DeviceIdType.MESH
        )

    above, below = lax.rem(ts + 1, ts_count), lax.rem(ts + ts_count - 1, ts_count)
    hops = [k for k in range(1, reach + 1) if k < ctx_count]
    pl.when(has_before)(lambda: greet(place(ahead)))
    pl.when(ts < ts_count - 1)(lambda: greet((ctx, above)))
    for k in hops:
        pl.when(ctx >= k)(lambda k=k: greet((lax.rem(ctx + ctx_count - k, ctx_count), ts)))
    peers = has_after.astype(jnp.int32) + (ts > 0).astype(jnp.int32)
    for k in hops:
        peers = peers + (ctx + k < ctx_count).astype(jnp.int32)
    pl.semaphore_wait(barrier, peers)

    main = copy(product, before, 0, place(after))
    chain = copy(run_out, run_in, 1, (ctx, above))
    suffix = copy(rest_out, rest_in, 2, (ctx, below))
    cross = [
        copy(whole_out, cross_in.at[k - 1], 2 + k, (lax.rem(ctx + k, ctx_count), ts))
        for k in hops
    ]
    to_end = (ts_count - 1 - ts).astype(jnp.float32)
    rest[...] = state[...] * faded(to_end, 1)
    entered[...] = jnp.zeros_like(entered)

    @pl.when(jnp.logical_not(has_before))
    def _():
        before[...] = jnp.zeros_like(before)

    pl.when(has_after)(main.start)

    def forward():
        @pl.when(ts > 0)
        def _():
            chain.wait_recv()
            entered[...] = run_in[...].astype(jnp.float32)

        @pl.when(ts < ts_count - 1)
        def _():
            run_out[...] = (state[...] + faded(1.0, 0) * entered[...]).astype(jnp.bfloat16)
            chain.start()

    def backward():
        @pl.when(ts < ts_count - 1)
        def _():
            suffix.wait_recv()
            rest[...] = rest[...] + rest_in[...].astype(jnp.float32)

        @pl.when(ts > 0)
        def _():
            rest_out[...] = rest[...].astype(jnp.bfloat16)
            suffix.start()

    late = ts >= ts_count // 2

    @pl.when(late)
    def _():
        backward()
        forward()

    @pl.when(jnp.logical_not(late))
    def _():
        forward()
        backward()

    whole_out[...] = (rest[...] + faded(to_end + 1.0, 2) * entered[...]).astype(jnp.bfloat16)
    for k, one in zip(hops, cross):
        pl.when(ctx + k < ctx_count)(one.start)
    for k, one in zip(hops, cross):
        @pl.when(ctx >= k)
        def _(k=k, one=one):
            one.wait_recv()
            distance = (ts + (k - 1) * ts_count).astype(jnp.float32)
            entered[...] = entered[...] + faded(distance, 2 + k) * cross_in[k - 1].astype(
                jnp.float32
            )
    pl.when(has_before)(main.wait_recv)
    pl.when(has_after)(main.wait_send)
    pl.when(ts < ts_count - 1)(chain.wait_send)
    pl.when(ts > 0)(suffix.wait_send)
    for k, one in zip(hops, cross):
        pl.when(ctx + k < ctx_count)(one.wait_send)


def block(shape, index):
    return pl.BlockSpec(shape, index)


def per_device(projected, doc_lengths, short_taps, medium_taps, decay_rates, residues, skip_gain):
    ts_count, ctx_count = lax.axis_size("ts"), lax.axis_size("ctx")
    ts_index, ctx_index = lax.axis_index("ts"), lax.axis_index("ctx")
    rows, width = projected.shape[0], projected.shape[1] // 3
    total = rows * ts_count * ctx_count
    span = rows * ts_count
    reach = -(-(total // 4) // span)
    devices = ts_count * ctx_count
    pairs = [(i, i + 1) for i in range(devices - 1)]
    everyone = ("ctx", "ts")
    tiles = width // TILE
    groups_tile = TILE // GROUP

    edge_kv = lax.ppermute(projected[rows - EDGE :, width:], everyone, pairs)
    edge_q = lax.ppermute(projected[rows - EDGE :, :width], everyone, pairs)

    begin = (ctx_index * ts_count + ts_index) * rows
    begin_array = jnp.full((1,), begin, jnp.int32)
    steps = jnp.arange(rows, dtype=jnp.float32)
    back = (rows - jnp.arange(rows)) % rows
    back_f = back.astype(jnp.float32)
    scaled = residues * jnp.sqrt(-jnp.expm1(-2.0 * decay_rates))
    medium_rows = jnp.concatenate([medium_taps[:1], medium_taps[:0:-1]], axis=0).T
    long_rows = jnp.sum(
        scaled[:, :, None] * jnp.exp(-decay_rates[:, :, None] * back_f[None, None]), axis=0
    )
    own_rows = medium_rows + long_rows
    rates_flat = decay_rates.T.reshape(-1)
    scaled_flat = scaled.T.reshape(-1)
    tail = jnp.exp(-rates_flat[:, None] * (rows - 1.0 - steps)[None, :]).astype(jnp.bfloat16)
    decay = (scaled_flat[None] * jnp.exp(-rates_flat[None] * (steps + 1.0)[:, None])).astype(
        jnp.bfloat16
    )
    taps = jnp.repeat(short_taps, GROUP, axis=2)
    rates_wide = lax.optimization_barrier(jnp.repeat(decay_rates, GROUP, axis=1))
    ends = jnp.cumsum(doc_lengths)
    begins = ends - doc_lengths

    def start_of(position):
        return jnp.max(jnp.where(begins <= position, begins, 0))

    last_own = start_of(begin + rows - 1)
    last_before = start_of(jnp.maximum(begin - 1, 0))
    span_begin = ctx_index * span
    last_span = start_of(span_begin + span - 1)
    edge_kv, edge_q, decay, own_rows, tail, taps, rates_wide, medium_rows, last_own, last_before, last_span = (
        lax.optimization_barrier(
            (edge_kv, edge_q, decay, own_rows, tail, taps, rates_wide, medium_rows, last_own, last_before, last_span)
        )
    )

    smem = pl.BlockSpec(memory_space=pltpu.SMEM)
    tile = lambda part=0: block((rows, TILE), lambda i: (0, i + part * tiles))
    edge = lambda part=0: block((EDGE, TILE), lambda i: (0, i + part * tiles))
    taps_tile = block((3, SHORT, TILE), lambda i: (0, 0, i))
    state_tile = block((MODES, TILE), lambda i: (0, i))
    wheel_tile = block((groups_tile, rows), lambda i: (i, 0))
    wide = lambda dtype: jax.ShapeDtypeStruct((rows, width), dtype)
    product, state = pl.pallas_call(
        product_kernel,
        grid=(tiles,),
        in_specs=[smem, smem, tile(1), tile(2), edge(0), edge(1), taps_tile,
                  block((TILE, rows), lambda i: (i, 0))],
        out_specs=[tile(), state_tile],
        out_shape=[wide(jnp.bfloat16), jax.ShapeDtypeStruct((MODES, width), jnp.float32)],
        scratch_shapes=[pltpu.VMEM((2, EDGE + rows, LANES), jnp.float32)],
        name="product",
    )(doc_lengths, begin_array, projected, projected, edge_kv, edge_kv, taps, tail)

    alive = [last_own < begin, last_span <= begin + rows - 1, last_span < begin] + [
        last_before <= span_begin - hop * span - 1 for hop in range(reach)
    ]
    flags = jnp.stack(alive).astype(jnp.float32)
    vmem = pl.BlockSpec(memory_space=pltpu.VMEM)
    held = pltpu.VMEM((MODES, width), jnp.bfloat16)
    before, entered = pl.pallas_call(
        functools.partial(exchange_kernel, ctx_count, ts_count, reach, rows),
        in_specs=[smem, vmem, vmem, vmem],
        out_specs=[vmem, vmem],
        out_shape=[wide(jnp.bfloat16), jax.ShapeDtypeStruct((MODES, width), jnp.float32)],
        scratch_shapes=[
            pltpu.VMEM((MODES, width), jnp.float32), held, held, held, held, held,
            pltpu.VMEM((reach, MODES, width), jnp.bfloat16),
            pltpu.SemaphoreType.DMA((3 + reach,)), pltpu.SemaphoreType.DMA((3 + reach,)),
        ],
        compiler_params=pltpu.CompilerParams(
            collective_id=0, has_side_effects=True, vmem_limit_bytes=32 * 2**20
        ),
        name="exchange",
    )(flags, product, state, rates_wide)

    partial, query = pl.pallas_call(
        local_kernel,
        grid=(tiles,),
        in_specs=[smem, smem, tile(), tile(), edge(), taps_tile, wheel_tile,
                  block((1, TILE), lambda i: (0, i))],
        out_specs=[tile(), tile()],
        out_shape=[wide(jnp.float32), wide(jnp.float32)],
        scratch_shapes=[
            pltpu.VMEM((EDGE + rows, LANES), jnp.float32),
            pltpu.VMEM((2, rows, PER * LANES), jnp.bfloat16),
        ],
        cost_estimate=pl.CostEstimate(
            flops=16 * rows * rows * width * PER, bytes_accessed=rows * width * 12, transcendentals=0
        ),
        name="local",
    )(doc_lengths, begin_array, product, projected, edge_q, taps, own_rows, skip_gain[None])

    return pl.pallas_call(
        final_kernel,
        grid=(tiles,),
        in_specs=[smem, smem, tile(), wheel_tile, tile(), state_tile, tile(), tile()],
        out_specs=tile(),
        out_shape=wide(jnp.bfloat16),
        scratch_shapes=[pltpu.VMEM((2, rows, PER * LANES), jnp.bfloat16)],
        name="final",
    )(doc_lengths, begin_array, before, medium_rows, decay, entered, partial, query)


def solution(mesh):
    return jax.shard_map(
        per_device,
        mesh=mesh,
        in_specs=(P(("ctx", "ts"), None), P(), P(), P(), P(), P(), P()),
        out_specs=P(("ctx", "ts"), None),
        check_vma=False,
    )
```

```python
import functools

import jax
import jax.numpy as jnp
from jax import lax
from jax.experimental import pallas as pl
from jax.experimental.pallas import tpu as pltpu
from jax.sharding import PartitionSpec as P

GROUP = 16
SHORT = 7
MODES = 16
LANES = 128
PER = LANES // GROUP
TILE = 512
EDGE = 8


def row_starts(lengths, begin, rows):
    position = begin + lax.broadcasted_iota(jnp.int32, (rows, LANES), 0)
    start = jnp.zeros((rows, LANES), jnp.int32)
    doc_begin = jnp.int32(0)
    for doc in range(lengths.shape[0]):
        start = jnp.where(position >= doc_begin, doc_begin, start)
        doc_begin = doc_begin + lengths[doc]
    return start, position


def short_conv(value, edge, taps, part, valid, window, lane):
    rows = value.shape[0]
    columns = pl.ds(pl.multiple_of(lane * LANES, LANES), LANES)
    window[pl.ds(0, EDGE), :] = edge[:, columns].astype(jnp.float32)
    window[pl.ds(EDGE, rows), :] = value[:, columns].astype(jnp.float32)
    total = window[pl.ds(EDGE, rows), :] * taps[part, 0:1, columns]
    for offset in range(1, SHORT):
        term = window[pl.ds(EDGE - offset, rows), :] * taps[part, offset : offset + 1, columns]
        total = total + jnp.where(valid >= offset, term, 0.0)
    return total


def on_diagonal(shape):
    row = lax.broadcasted_iota(jnp.int32, shape, 0) // GROUP
    column = lax.broadcasted_iota(jnp.int32, shape, 1) // GROUP
    return row == column


def spread(block):
    lane_group = lax.broadcasted_iota(jnp.int32, (1, LANES), 1) // GROUP
    parts = [jnp.where(lane_group == g, block, 0.0) for g in range(PER)]
    return jnp.concatenate(parts, axis=0).astype(jnp.bfloat16)


def circulants(rows_ref, lane, mask, band):
    for g in range(PER):
        taps = rows_ref[pl.ds(lane * PER + g, 1), :]
        wheel = pltpu.roll(
            jnp.broadcast_to(taps, (LANES, LANES)), 0, 1, stride=1, stride_axis=0
        )
        band[:, pl.ds(g * LANES, LANES)] = jnp.where(mask, wheel, 0.0).astype(jnp.bfloat16)


def product_kernel(lengths, begin, k_ref, v_ref, ke_ref, ve_ref, taps, tail, out, state, window):
    rows = k_ref.shape[0]
    start, position = row_starts(lengths, begin[0], rows)
    valid = position - start
    last = jnp.max(start)
    diagonal = on_diagonal((LANES, LANES))
    for lane in range(TILE // LANES):
        columns = pl.ds(lane * LANES, LANES)
        key = short_conv(k_ref, ke_ref, taps, 1, valid, window.at[0], lane)
        value = short_conv(v_ref, ve_ref, taps, 2, valid, window.at[1], lane)
        product = (key * value).astype(jnp.bfloat16)
        out[:, columns] = product
        kept = jnp.where(position >= last, product.astype(jnp.float32), 0.0).astype(jnp.bfloat16)
        full = jnp.dot(tail[columns, :], kept, preferred_element_type=jnp.float32)
        full = jnp.where(diagonal, full, 0.0)
        summed = full[0:MODES]
        for g in range(1, PER):
            summed = summed + full[g * MODES : (g + 1) * MODES]
        state[:, columns] = summed


def local_part(lengths, begin, x_ref, q_ref, qe_ref, taps, wheel, skip, partial, query, window, band):
    rows, width = x_ref.shape
    start, position = row_starts(lengths, begin, rows)
    valid = position - start
    row = lax.broadcasted_iota(jnp.int32, (rows, LANES), 0)
    column = lax.broadcasted_iota(jnp.int32, (rows, LANES), 1)
    mask = (column <= row) & (column + begin >= start)

    def one(lane, carry):
        columns = pl.ds(pl.multiple_of(lane * LANES, LANES), LANES)
        query[:, columns] = short_conv(q_ref, qe_ref, taps, 0, valid, window, lane)
        block = x_ref[:, columns].astype(jnp.float32)
        circulants(wheel, lane, mask, band)
        summed = jnp.dot(band[...], spread(block), preferred_element_type=jnp.float32)
        partial[:, columns] = summed + skip[:, columns] * block
        return carry

    lax.fori_loop(0, width // LANES, one, 0)


def final_kernel(
    lengths, begin, x_ref, wheel, decay, state, partial, query, out, band
):
    rows = x_ref.shape[0]
    start, position = row_starts(lengths, begin[0], rows)
    row = lax.broadcasted_iota(jnp.int32, (rows, LANES), 0)
    column = lax.broadcasted_iota(jnp.int32, (rows, LANES), 1)
    mask = (column > row) & (column + (begin[0] - rows) >= start)
    carried_rows = start < begin[0]
    diagonal = on_diagonal((LANES, LANES))
    for lane in range(TILE // LANES):
        columns = pl.ds(lane * LANES, LANES)
        block = x_ref[:, columns].astype(jnp.float32)
        circulants(wheel, lane, mask, band.at[lane % 2])
        summed = jnp.dot(band[lane % 2], spread(block), preferred_element_type=jnp.float32)
        stacked = jnp.concatenate([state[:, columns]] * PER, axis=0)
        stacked = jnp.where(diagonal, stacked, 0.0).astype(jnp.bfloat16)
        carried = jnp.dot(decay[:, columns], stacked, preferred_element_type=jnp.float32)
        carried = jnp.where(carried_rows, carried, 0.0)
        filtered = (partial[:, columns] + summed + carried).astype(jnp.bfloat16)
        out[:, columns] = (query[:, columns] * filtered.astype(jnp.float32)).astype(jnp.bfloat16)


def exchange_kernel(
    ctx_count, ts_count, reach, rows, lengths, flags, product, state, rates, q_ref, qe_ref, taps,
    wheel, skip, before, entered, partial, query, window, band,
    rest, run_out, run_in, rest_out, rest_in, whole_out, cross_in, send, recv
):
    ctx, ts = lax.axis_index("ctx"), lax.axis_index("ts")
    me = ctx * ts_count + ts
    has_before, has_after = me > 0, me < ctx_count * ts_count - 1
    after, ahead = me + 1, me - 1 + ctx_count * ts_count

    def place(index):
        return (lax.rem(lax.div(index, ts_count), ctx_count), lax.rem(index, ts_count))

    def copy(source, target, slot, device):
        return pltpu.make_async_remote_copy(
            src_ref=source, dst_ref=target, send_sem=send.at[slot], recv_sem=recv.at[slot],
            device_id=device, device_id_type=pl.DeviceIdType.MESH,
        )

    def faded(distance, flag):
        return jnp.exp(rates[...] * (-jnp.float32(rows) * distance)) * flags[flag]

    barrier = pltpu.get_barrier_semaphore()

    def greet(device):
        pl.semaphore_signal(
            barrier, inc=1, device_id=device, device_id_type=pl.DeviceIdType.MESH
        )

    above, below = lax.rem(ts + 1, ts_count), lax.rem(ts + ts_count - 1, ts_count)
    hops = [k for k in range(1, reach + 1) if k < ctx_count]
    pl.when(has_before)(lambda: greet(place(ahead)))
    pl.when(ts < ts_count - 1)(lambda: greet((ctx, above)))
    for k in hops:
        pl.when(ctx >= k)(lambda k=k: greet((lax.rem(ctx + ctx_count - k, ctx_count), ts)))
    peers = has_after.astype(jnp.int32) + (ts > 0).astype(jnp.int32)
    for k in hops:
        peers = peers + (ctx + k < ctx_count).astype(jnp.int32)
    pl.semaphore_wait(barrier, peers)

    half = rows // 2
    first, second = pl.ds(0, half), pl.ds(half, half)
    main = copy(product.at[first], before.at[first], 0, place(after))
    other = copy(product.at[second], before.at[second], 3 + reach, place(after))
    chain = copy(run_out, run_in, 1, (ctx, above))
    suffix = copy(rest_out, rest_in, 2, (ctx, below))
    cross = [
        copy(whole_out, cross_in.at[k - 1], 2 + k, (lax.rem(ctx + k, ctx_count), ts))
        for k in hops
    ]
    to_end = (ts_count - 1 - ts).astype(jnp.float32)
    rest[...] = state[...] * faded(to_end, 1)
    entered[...] = jnp.zeros_like(entered)

    @pl.when(jnp.logical_not(has_before))
    def _():
        before[...] = jnp.zeros_like(before)

    def forward():
        @pl.when(ts > 0)
        def _():
            chain.wait_recv()
            entered[...] = run_in[...].astype(jnp.float32)

        @pl.when(ts < ts_count - 1)
        def _():
            run_out[...] = (state[...] + faded(1.0, 0) * entered[...]).astype(jnp.bfloat16)
            chain.start()

    def backward():
        @pl.when(ts < ts_count - 1)
        def _():
            suffix.wait_recv()
            rest[...] = rest[...] + rest_in[...].astype(jnp.float32)

        @pl.when(ts > 0)
        def _():
            rest_out[...] = rest[...].astype(jnp.bfloat16)
            suffix.start()

    bottom, top = ts == 0, ts == ts_count - 1
    late = ts >= ts_count // 2
    pl.when(bottom)(forward)
    pl.when(top)(backward)
    pl.when(has_after)(main.start)
    local_part(
        lengths, me * rows, product, q_ref, qe_ref, taps, wheel, skip, partial, query, window, band
    )

    @pl.when(late)
    def _():
        pl.when(jnp.logical_not(top))(backward)
        forward()

    @pl.when(jnp.logical_not(late))
    def _():
        pl.when(jnp.logical_not(bottom))(forward)
        backward()

    whole_out[...] = (rest[...] + faded(to_end + 1.0, 2) * entered[...]).astype(jnp.bfloat16)
    for k, one in zip(hops, cross):
        pl.when(ctx + k < ctx_count)(one.start)
    pl.when(has_after)(other.start)
    for k, one in zip(hops, cross):
        @pl.when(ctx >= k)
        def _(k=k, one=one):
            one.wait_recv()
            distance = (ts + (k - 1) * ts_count).astype(jnp.float32)
            entered[...] = entered[...] + faded(distance, 2 + k) * cross_in[k - 1].astype(
                jnp.float32
            )
    for one in (main, other):
        pl.when(has_before)(one.wait_recv)
        pl.when(has_after)(one.wait_send)
    pl.when(ts < ts_count - 1)(chain.wait_send)
    pl.when(ts > 0)(suffix.wait_send)
    for k, one in zip(hops, cross):
        pl.when(ctx + k < ctx_count)(one.wait_send)


def block(shape, index):
    return pl.BlockSpec(shape, index)


def per_device(projected, doc_lengths, short_taps, medium_taps, decay_rates, residues, skip_gain):
    ts_count, ctx_count = lax.axis_size("ts"), lax.axis_size("ctx")
    ts_index, ctx_index = lax.axis_index("ts"), lax.axis_index("ctx")
    rows, width = projected.shape[0], projected.shape[1] // 3
    total = rows * ts_count * ctx_count
    span = rows * ts_count
    reach = -(-(total // 4) // span)
    devices = ts_count * ctx_count
    pairs = [(i, i + 1) for i in range(devices - 1)]
    everyone = ("ctx", "ts")
    tiles = width // TILE
    groups_tile = TILE // GROUP

    edges = lax.ppermute(projected[rows - EDGE :], everyone, pairs)

    begin = (ctx_index * ts_count + ts_index) * rows
    begin_array = jnp.full((1,), begin, jnp.int32)
    steps = jnp.arange(rows, dtype=jnp.float32)
    back = (rows - jnp.arange(rows)) % rows
    back_f = back.astype(jnp.float32)
    scaled = residues * jnp.sqrt(-jnp.expm1(-2.0 * decay_rates))
    medium_rows = jnp.concatenate([medium_taps[:1], medium_taps[:0:-1]], axis=0).T
    long_rows = jnp.sum(
        scaled[:, :, None] * jnp.exp(-decay_rates[:, :, None] * back_f[None, None]), axis=0
    )
    own_rows = medium_rows + long_rows
    rates_flat = decay_rates.T.reshape(-1)
    scaled_flat = scaled.T.reshape(-1)
    tail = jnp.exp(-rates_flat[:, None] * (rows - 1.0 - steps)[None, :]).astype(jnp.bfloat16)
    decay = (scaled_flat[None] * jnp.exp(-rates_flat[None] * (steps + 1.0)[:, None])).astype(
        jnp.bfloat16
    )
    taps = jnp.repeat(short_taps, GROUP, axis=2)
    rates_wide = lax.optimization_barrier(jnp.repeat(decay_rates, GROUP, axis=1))
    ends = jnp.cumsum(doc_lengths)
    begins = ends - doc_lengths

    def start_of(position):
        return jnp.max(jnp.where(begins <= position, begins, 0))

    last_own = start_of(begin + rows - 1)
    last_before = start_of(jnp.maximum(begin - 1, 0))
    span_begin = ctx_index * span
    last_span = start_of(span_begin + span - 1)
    edges, decay, own_rows, tail, taps, rates_wide, medium_rows, last_own, last_before, last_span = (
        lax.optimization_barrier(
            (edges, decay, own_rows, tail, taps, rates_wide, medium_rows, last_own, last_before, last_span)
        )
    )

    smem = pl.BlockSpec(memory_space=pltpu.SMEM)
    tile = lambda part=0: block((rows, TILE), lambda i: (0, i + part * tiles))
    edge = lambda part=0: block((EDGE, TILE), lambda i: (0, i + part * tiles))
    taps_tile = block((3, SHORT, TILE), lambda i: (0, 0, i))
    state_tile = block((MODES, TILE), lambda i: (0, i))
    wheel_tile = block((groups_tile, rows), lambda i: (i, 0))
    wide = lambda dtype: jax.ShapeDtypeStruct((rows, width), dtype)
    product, state = pl.pallas_call(
        product_kernel,
        grid=(tiles,),
        in_specs=[smem, smem, tile(1), tile(2), edge(1), edge(2), taps_tile,
                  block((TILE, rows), lambda i: (i, 0))],
        out_specs=[tile(), state_tile],
        out_shape=[wide(jnp.bfloat16), jax.ShapeDtypeStruct((MODES, width), jnp.float32)],
        scratch_shapes=[pltpu.VMEM((2, EDGE + rows, LANES), jnp.float32)],
        name="product",
    )(doc_lengths, begin_array, projected, projected, edges, edges, taps, tail)

    alive = [last_own < begin, last_span <= begin + rows - 1, last_span < begin] + [
        last_before <= span_begin - hop * span - 1 for hop in range(reach)
    ]
    flags = jnp.stack(alive).astype(jnp.float32)
    vmem = pl.BlockSpec(memory_space=pltpu.VMEM)
    held = pltpu.VMEM((MODES, width), jnp.bfloat16)
    before, entered, partial, query = pl.pallas_call(
        functools.partial(exchange_kernel, ctx_count, ts_count, reach, rows),
        grid=(1,),
        in_specs=[smem, smem, vmem, vmem, vmem, block((rows, width), lambda i: (0, 0)),
                  block((EDGE, width), lambda i: (0, 0)), vmem, vmem, vmem],
        out_specs=[vmem, vmem, vmem, vmem],
        out_shape=[wide(jnp.bfloat16), jax.ShapeDtypeStruct((MODES, width), jnp.float32),
                   wide(jnp.float32), wide(jnp.float32)],
        scratch_shapes=[
            pltpu.VMEM((EDGE + rows, LANES), jnp.float32),
            pltpu.VMEM((rows, PER * LANES), jnp.bfloat16),
            pltpu.VMEM((MODES, width), jnp.float32), held, held, held, held, held,
            pltpu.VMEM((reach, MODES, width), jnp.bfloat16),
            pltpu.SemaphoreType.DMA((4 + reach,)), pltpu.SemaphoreType.DMA((4 + reach,)),
        ],
        compiler_params=pltpu.CompilerParams(
            collective_id=0, has_side_effects=True, vmem_limit_bytes=32 * 2**20
        ),
        name="exchange",
    )(doc_lengths, flags, product, state, rates_wide, projected, edges, taps, own_rows, skip_gain[None])

    return pl.pallas_call(
        final_kernel,
        grid=(tiles,),
        in_specs=[smem, smem, tile(), wheel_tile, tile(), state_tile, tile(), tile()],
        out_specs=tile(),
        out_shape=wide(jnp.bfloat16),
        scratch_shapes=[pltpu.VMEM((2, rows, PER * LANES), jnp.bfloat16)],
        name="final",
    )(doc_lengths, begin_array, before, medium_rows, decay, entered, partial, query)


def solution(mesh):
    return jax.shard_map(
        per_device,
        mesh=mesh,
        in_specs=(P(("ctx", "ts"), None), P(), P(), P(), P(), P(), P()),
        out_specs=P(("ctx", "ts"), None),
        check_vma=False,
    )
```

```python
import functools

import jax
import jax.numpy as jnp
from jax import lax
from jax.experimental import pallas as pl
from jax.experimental.pallas import tpu as pltpu
from jax.sharding import PartitionSpec as P

GROUP = 16
SHORT = 7
MODES = 16
LANES = 128
PER = LANES // GROUP
TILE = 512
EDGE = 8


def row_starts(lengths, begin, rows):
    position = begin + lax.broadcasted_iota(jnp.int32, (rows, LANES), 0)
    start = jnp.zeros((rows, LANES), jnp.int32)
    doc_begin = jnp.int32(0)
    for doc in range(lengths.shape[0]):
        start = jnp.where(position >= doc_begin, doc_begin, start)
        doc_begin = doc_begin + lengths[doc]
    return start, position


def short_conv(value, edge, taps, part, valid, window, lane):
    rows = value.shape[0]
    columns = pl.ds(lane * LANES, LANES)
    window[pl.ds(0, EDGE), :] = edge[:, columns].astype(jnp.float32)
    window[pl.ds(EDGE, rows), :] = value[:, columns].astype(jnp.float32)
    total = window[pl.ds(EDGE, rows), :] * taps[part, 0:1, columns]
    for offset in range(1, SHORT):
        term = window[pl.ds(EDGE - offset, rows), :] * taps[part, offset : offset + 1, columns]
        total = total + jnp.where(valid >= offset, term, 0.0)
    return total


def on_diagonal(shape):
    row = lax.broadcasted_iota(jnp.int32, shape, 0) // GROUP
    column = lax.broadcasted_iota(jnp.int32, shape, 1) // GROUP
    return row == column


def spread(block):
    lane_group = lax.broadcasted_iota(jnp.int32, (1, LANES), 1) // GROUP
    parts = [jnp.where(lane_group == g, block, 0.0) for g in range(PER)]
    return jnp.concatenate(parts, axis=0).astype(jnp.bfloat16)


def circulants(rows_ref, lane, mask, band):
    for g in range(PER):
        taps = rows_ref[pl.ds(lane * PER + g, 1), :]
        wheel = pltpu.roll(
            jnp.broadcast_to(taps, (LANES, LANES)), 0, 1, stride=1, stride_axis=0
        )
        band[:, pl.ds(g * LANES, LANES)] = jnp.where(mask, wheel, 0.0).astype(jnp.bfloat16)


def product_kernel(lengths, begin, k_ref, v_ref, ke_ref, ve_ref, taps, tail, out, state, window):
    rows = k_ref.shape[0]
    start, position = row_starts(lengths, begin[0], rows)
    valid = position - start
    last = jnp.max(start)
    diagonal = on_diagonal((LANES, LANES))
    for lane in range(TILE // LANES):
        columns = pl.ds(lane * LANES, LANES)
        key = short_conv(k_ref, ke_ref, taps, 1, valid, window.at[0], lane)
        value = short_conv(v_ref, ve_ref, taps, 2, valid, window.at[1], lane)
        product = (key * value).astype(jnp.bfloat16)
        out[:, columns] = product
        kept = jnp.where(position >= last, product.astype(jnp.float32), 0.0).astype(jnp.bfloat16)
        full = jnp.dot(tail[columns, :], kept, preferred_element_type=jnp.float32)
        full = jnp.where(diagonal, full, 0.0)
        summed = full[0:MODES]
        for g in range(1, PER):
            summed = summed + full[g * MODES : (g + 1) * MODES]
        state[:, columns] = summed


def local_kernel(
    lengths, begin, x_ref, q_ref, qe_ref, taps, wheel, skip, partial, query, window, band
):
    rows = x_ref.shape[0]
    start, position = row_starts(lengths, begin[0], rows)
    valid = position - start
    row = lax.broadcasted_iota(jnp.int32, (rows, LANES), 0)
    column = lax.broadcasted_iota(jnp.int32, (rows, LANES), 1)
    mask = (column <= row) & (column + begin[0] >= start)
    for lane in range(TILE // LANES):
        columns = pl.ds(lane * LANES, LANES)
        query[:, columns] = short_conv(q_ref, qe_ref, taps, 0, valid, window, lane)
        block = x_ref[:, columns].astype(jnp.float32)
        circulants(wheel, lane, mask, band.at[lane % 2])
        summed = jnp.dot(band[lane % 2], spread(block), preferred_element_type=jnp.float32)
        partial[:, columns] = summed + skip[:, columns] * block


def final_kernel(
    lengths, begin, x_ref, wheel, decay, state, partial, query, out, band
):
    rows = x_ref.shape[0]
    start, position = row_starts(lengths, begin[0], rows)
    row = lax.broadcasted_iota(jnp.int32, (rows, LANES), 0)
    column = lax.broadcasted_iota(jnp.int32, (rows, LANES), 1)
    mask = (column > row) & (column + (begin[0] - rows) >= start)
    carried_rows = start < begin[0]
    diagonal = on_diagonal((LANES, LANES))
    for lane in range(TILE // LANES):
        columns = pl.ds(lane * LANES, LANES)
        block = x_ref[:, columns].astype(jnp.float32)
        circulants(wheel, lane, mask, band.at[lane % 2])
        summed = jnp.dot(band[lane % 2], spread(block), preferred_element_type=jnp.float32)
        stacked = jnp.concatenate([state[:, columns]] * PER, axis=0)
        stacked = jnp.where(diagonal, stacked, 0.0).astype(jnp.bfloat16)
        carried = jnp.dot(decay[:, columns], stacked, preferred_element_type=jnp.float32)
        carried = jnp.where(carried_rows, carried, 0.0)
        filtered = (partial[:, columns] + summed + carried).astype(jnp.bfloat16)
        out[:, columns] = (query[:, columns] * filtered.astype(jnp.float32)).astype(jnp.bfloat16)


def block(shape, index):
    return pl.BlockSpec(shape, index)


def per_device(projected, doc_lengths, short_taps, medium_taps, decay_rates, residues, skip_gain):
    ts_count, ctx_count = lax.axis_size("ts"), lax.axis_size("ctx")
    ts_index, ctx_index = lax.axis_index("ts"), lax.axis_index("ctx")
    rows, width = projected.shape[0], projected.shape[1] // 3
    total = rows * ts_count * ctx_count
    span = rows * ts_count
    reach = -(-(total // 4) // span)
    devices = ts_count * ctx_count
    pairs = [(i, i + 1) for i in range(devices - 1)]
    everyone = ("ctx", "ts")
    tiles = width // TILE
    groups_tile = TILE // GROUP

    edges = lax.ppermute(projected[rows - EDGE :], everyone, pairs)

    begin = (ctx_index * ts_count + ts_index) * rows
    begin_array = jnp.full((1,), begin, jnp.int32)
    steps = jnp.arange(rows, dtype=jnp.float32)
    back = (rows - jnp.arange(rows)) % rows
    back_f = back.astype(jnp.float32)
    scaled = residues * jnp.sqrt(-jnp.expm1(-2.0 * decay_rates))
    medium_rows = jnp.concatenate([medium_taps[:1], medium_taps[:0:-1]], axis=0).T
    long_rows = jnp.sum(
        scaled[:, :, None] * jnp.exp(-decay_rates[:, :, None] * back_f[None, None]), axis=0
    )
    own_rows = medium_rows + long_rows
    rates_flat = decay_rates.T.reshape(-1)
    scaled_flat = scaled.T.reshape(-1)
    tail = jnp.exp(-rates_flat[:, None] * (rows - 1.0 - steps)[None, :]).astype(jnp.bfloat16)
    decay = (scaled_flat[None] * jnp.exp(-rates_flat[None] * (steps + 1.0)[:, None])).astype(
        jnp.bfloat16
    )
    taps = jnp.repeat(short_taps, GROUP, axis=2)
    rates_wide = lax.optimization_barrier(jnp.repeat(decay_rates, GROUP, axis=1))

    smem = pl.BlockSpec(memory_space=pltpu.SMEM)
    tile = lambda part=0: block((rows, TILE), lambda i: (0, i + part * tiles))
    edge = lambda part=0: block((EDGE, TILE), lambda i: (0, i + part * tiles))
    taps_tile = block((3, SHORT, TILE), lambda i: (0, 0, i))
    state_tile = block((MODES, TILE), lambda i: (0, i))
    wheel_tile = block((groups_tile, rows), lambda i: (i, 0))
    wide = lambda dtype: jax.ShapeDtypeStruct((rows, width), dtype)
    product, state = pl.pallas_call(
        product_kernel,
        grid=(tiles,),
        in_specs=[smem, smem, tile(1), tile(2), edge(1), edge(2), taps_tile,
                  block((TILE, rows), lambda i: (i, 0))],
        out_specs=[tile(), state_tile],
        out_shape=[wide(jnp.bfloat16), jax.ShapeDtypeStruct((MODES, width), jnp.float32)],
        scratch_shapes=[pltpu.VMEM((2, EDGE + rows, LANES), jnp.float32)],
        name="product",
    )(doc_lengths, begin_array, projected, projected, edges, edges, taps, tail)

    before = lax.ppermute(product, everyone, pairs)

    ends = jnp.cumsum(doc_lengths)
    begins = ends - doc_lengths

    def start_of(position):
        return jnp.max(jnp.where(begins <= position, begins, 0))

    def faded(distance, alive):
        return jnp.where(alive, jnp.exp(-rates_wide * (distance * jnp.float32(rows))), 0.0)

    last_own = start_of(begin + rows - 1)
    last_before = start_of(jnp.maximum(begin - 1, 0))
    span_begin = ctx_index * span
    last_span = start_of(span_begin + span - 1)
    to_end = (ts_count - 1 - ts_index).astype(jnp.float32)
    step_in = faded(1.0, last_own < begin)
    running, entered = state, jnp.zeros_like(state)
    rest = state * faded(to_end, last_span <= begin + rows - 1)
    for hop in range(ts_count - 1):
        got = lax.ppermute(running.astype(jnp.bfloat16), "ts", [(hop, hop + 1)])
        back_hop = ts_count - 1 - hop
        got_rest = lax.ppermute(rest.astype(jnp.bfloat16), "ts", [(back_hop, back_hop - 1)])
        got = got.astype(jnp.float32)
        entered = entered + got
        running = running + step_in * got
        rest = rest + got_rest.astype(jnp.float32)
    whole = rest + faded(to_end + 1.0, last_span < begin) * entered
    whole = whole.astype(jnp.bfloat16)
    for hop in range(1, reach + 1):
        if hop >= ctx_count:
            break
        got = lax.ppermute(whole, "ctx", [(i, i + hop) for i in range(ctx_count - hop)])
        distance = (ts_index + (hop - 1) * ts_count).astype(jnp.float32)
        alive = last_before <= span_begin - (hop - 1) * span - 1
        entered = entered + faded(distance, alive) * got.astype(jnp.float32)

    partial, query = pl.pallas_call(
        local_kernel,
        grid=(tiles,),
        in_specs=[smem, smem, tile(), tile(), edge(), taps_tile, wheel_tile,
                  block((1, TILE), lambda i: (0, i))],
        out_specs=[tile(), tile()],
        out_shape=[wide(jnp.float32), wide(jnp.float32)],
        scratch_shapes=[
            pltpu.VMEM((EDGE + rows, LANES), jnp.float32),
            pltpu.VMEM((2, rows, PER * LANES), jnp.bfloat16),
        ],
        cost_estimate=pl.CostEstimate(
            flops=2 * rows * rows * width * PER, bytes_accessed=rows * width * 12, transcendentals=0
        ),
        name="local",
    )(doc_lengths, begin_array, product, projected, edges, taps, own_rows, skip_gain[None])

    return pl.pallas_call(
        final_kernel,
        grid=(tiles,),
        in_specs=[smem, smem, tile(), wheel_tile, tile(), state_tile, tile(), tile()],
        out_specs=tile(),
        out_shape=wide(jnp.bfloat16),
        scratch_shapes=[pltpu.VMEM((2, rows, PER * LANES), jnp.bfloat16)],
        name="final",
    )(doc_lengths, begin_array, before, medium_rows, decay, entered, partial, query)


def solution(mesh):
    return jax.shard_map(
        per_device,
        mesh=mesh,
        in_specs=(P(("ctx", "ts"), None), P(), P(), P(), P(), P(), P()),
        out_specs=P(("ctx", "ts"), None),
        check_vma=False,
    )
```

```python
import functools

import jax
import jax.numpy as jnp
from jax import lax
from jax.experimental import pallas as pl
from jax.experimental.pallas import tpu as pltpu
from jax.sharding import PartitionSpec as P

GROUP = 16
SHORT = 7
MODES = 16
LANES = 128
PER = LANES // GROUP
TILE = 512
EDGE = 8


def row_starts(lengths, begin, rows):
    position = begin + lax.broadcasted_iota(jnp.int32, (rows, LANES), 0)
    start = jnp.zeros((rows, LANES), jnp.int32)
    doc_begin = jnp.int32(0)
    for doc in range(lengths.shape[0]):
        start = jnp.where(position >= doc_begin, doc_begin, start)
        doc_begin = doc_begin + lengths[doc]
    return start, position


def short_conv(value, edge, taps, part, valid, window, lane):
    rows = value.shape[0]
    columns = pl.ds(lane * LANES, LANES)
    window[pl.ds(0, EDGE), :] = edge[:, columns].astype(jnp.float32)
    window[pl.ds(EDGE, rows), :] = value[:, columns].astype(jnp.float32)
    total = window[pl.ds(EDGE, rows), :] * taps[part, 0:1, columns]
    for offset in range(1, SHORT):
        term = window[pl.ds(EDGE - offset, rows), :] * taps[part, offset : offset + 1, columns]
        total = total + jnp.where(valid >= offset, term, 0.0)
    return total


def on_diagonal(shape):
    row = lax.broadcasted_iota(jnp.int32, shape, 0) // GROUP
    column = lax.broadcasted_iota(jnp.int32, shape, 1) // GROUP
    return row == column


def spread(block):
    lane_group = lax.broadcasted_iota(jnp.int32, (1, LANES), 1) // GROUP
    parts = [jnp.where(lane_group == g, block, 0.0) for g in range(PER)]
    return jnp.concatenate(parts, axis=0).astype(jnp.bfloat16)


def circulants(rows_ref, lane, mask, band):
    for g in range(PER):
        taps = rows_ref[pl.ds(lane * PER + g, 1), :]
        wheel = pltpu.roll(
            jnp.broadcast_to(taps, (LANES, LANES)), 0, 1, stride=1, stride_axis=0
        )
        band[:, pl.ds(g * LANES, LANES)] = jnp.where(mask, wheel, 0.0).astype(jnp.bfloat16)


def product_kernel(lengths, begin, k_ref, v_ref, ke_ref, ve_ref, taps, tail, out, state, window):
    rows = k_ref.shape[0]
    start, position = row_starts(lengths, begin[0], rows)
    valid = position - start
    last = jnp.max(start)
    diagonal = on_diagonal((LANES, LANES))
    for lane in range(TILE // LANES):
        columns = pl.ds(lane * LANES, LANES)
        key = short_conv(k_ref, ke_ref, taps, 1, valid, window.at[0], lane)
        value = short_conv(v_ref, ve_ref, taps, 2, valid, window.at[1], lane)
        product = (key * value).astype(jnp.bfloat16)
        out[:, columns] = product
        kept = jnp.where(position >= last, product.astype(jnp.float32), 0.0).astype(jnp.bfloat16)
        full = jnp.dot(tail[columns, :], kept, preferred_element_type=jnp.float32)
        full = jnp.where(diagonal, full, 0.0)
        summed = full[0:MODES]
        for g in range(1, PER):
            summed = summed + full[g * MODES : (g + 1) * MODES]
        state[:, columns] = summed


def local_kernel(
    lengths, begin, x_ref, q_ref, qe_ref, taps, wheel, skip, partial, query, window, band
):
    rows = x_ref.shape[0]
    start, position = row_starts(lengths, begin[0], rows)
    valid = position - start
    row = lax.broadcasted_iota(jnp.int32, (rows, LANES), 0)
    column = lax.broadcasted_iota(jnp.int32, (rows, LANES), 1)
    mask = (column <= row) & (column + begin[0] >= start)
    for lane in range(TILE // LANES):
        columns = pl.ds(lane * LANES, LANES)
        query[:, columns] = short_conv(q_ref, qe_ref, taps, 0, valid, window, lane)
        block = x_ref[:, columns].astype(jnp.float32)
        circulants(wheel, lane, mask, band.at[lane % 2])
        summed = jnp.dot(band[lane % 2], spread(block), preferred_element_type=jnp.float32)
        partial[:, columns] = summed + skip[:, columns] * block


def final_kernel(
    lengths, begin, x_ref, wheel, decay, state, partial, query, out, band
):
    rows = x_ref.shape[0]
    start, position = row_starts(lengths, begin[0], rows)
    row = lax.broadcasted_iota(jnp.int32, (rows, LANES), 0)
    column = lax.broadcasted_iota(jnp.int32, (rows, LANES), 1)
    mask = (column > row) & (column + (begin[0] - rows) >= start)
    carried_rows = start < begin[0]
    diagonal = on_diagonal((LANES, LANES))
    for lane in range(TILE // LANES):
        columns = pl.ds(lane * LANES, LANES)
        block = x_ref[:, columns].astype(jnp.float32)
        circulants(wheel, lane, mask, band.at[lane % 2])
        summed = jnp.dot(band[lane % 2], spread(block), preferred_element_type=jnp.float32)
        stacked = jnp.concatenate([state[:, columns]] * PER, axis=0)
        stacked = jnp.where(diagonal, stacked, 0.0).astype(jnp.bfloat16)
        carried = jnp.dot(decay[:, columns], stacked, preferred_element_type=jnp.float32)
        carried = jnp.where(carried_rows, carried, 0.0)
        filtered = (partial[:, columns] + summed + carried).astype(jnp.bfloat16)
        out[:, columns] = (query[:, columns] * filtered.astype(jnp.float32)).astype(jnp.bfloat16)


def block(shape, index):
    return pl.BlockSpec(shape, index)


def per_device(projected, doc_lengths, short_taps, medium_taps, decay_rates, residues, skip_gain):
    ts_count, ctx_count = lax.axis_size("ts"), lax.axis_size("ctx")
    ts_index, ctx_index = lax.axis_index("ts"), lax.axis_index("ctx")
    rows, width = projected.shape[0], projected.shape[1] // 3
    total = rows * ts_count * ctx_count
    span = rows * ts_count
    reach = -(-(total // 4) // span)
    devices = ts_count * ctx_count
    pairs = [(i, i + 1) for i in range(devices - 1)]
    everyone = ("ctx", "ts")
    tiles = width // TILE
    groups_tile = TILE // GROUP

    edges = lax.ppermute(projected[rows - EDGE :], everyone, pairs)

    begin = (ctx_index * ts_count + ts_index) * rows
    begin_array = jnp.full((1,), begin, jnp.int32)
    steps = jnp.arange(rows, dtype=jnp.float32)
    back = (rows - jnp.arange(rows)) % rows
    back_f = back.astype(jnp.float32)
    scaled = residues * jnp.sqrt(-jnp.expm1(-2.0 * decay_rates))
    medium_rows = jnp.concatenate([medium_taps[:1], medium_taps[:0:-1]], axis=0).T
    long_rows = jnp.sum(
        scaled[:, :, None] * jnp.exp(-decay_rates[:, :, None] * back_f[None, None]), axis=0
    )
    own_rows = medium_rows + long_rows
    rates_flat = decay_rates.T.reshape(-1)
    scaled_flat = scaled.T.reshape(-1)
    tail = jnp.exp(-rates_flat[:, None] * (rows - 1.0 - steps)[None, :]).astype(jnp.bfloat16)
    decay = (scaled_flat[None] * jnp.exp(-rates_flat[None] * (steps + 1.0)[:, None])).astype(
        jnp.bfloat16
    )
    taps = jnp.repeat(short_taps, GROUP, axis=2)
    rates_wide = jnp.repeat(decay_rates, GROUP, axis=1)

    smem = pl.BlockSpec(memory_space=pltpu.SMEM)
    tile = lambda part=0: block((rows, TILE), lambda i: (0, i + part * tiles))
    edge = lambda part=0: block((EDGE, TILE), lambda i: (0, i + part * tiles))
    taps_tile = block((3, SHORT, TILE), lambda i: (0, 0, i))
    state_tile = block((MODES, TILE), lambda i: (0, i))
    wheel_tile = block((groups_tile, rows), lambda i: (i, 0))
    wide = lambda dtype: jax.ShapeDtypeStruct((rows, width), dtype)
    product, state = pl.pallas_call(
        product_kernel,
        grid=(tiles,),
        in_specs=[smem, smem, tile(1), tile(2), edge(1), edge(2), taps_tile,
                  block((TILE, rows), lambda i: (i, 0))],
        out_specs=[tile(), state_tile],
        out_shape=[wide(jnp.bfloat16), jax.ShapeDtypeStruct((MODES, width), jnp.float32)],
        scratch_shapes=[pltpu.VMEM((2, EDGE + rows, LANES), jnp.float32)],
        name="product",
    )(doc_lengths, begin_array, projected, projected, edges, edges, taps, tail)

    before = lax.ppermute(product, everyone, pairs)

    ends = jnp.cumsum(doc_lengths)
    begins = ends - doc_lengths

    def start_of(position):
        return jnp.max(jnp.where(begins <= position, begins, 0))

    def faded(distance, alive):
        return jnp.where(alive, jnp.exp(-rates_wide * (distance * jnp.float32(rows))), 0.0)

    last_own = start_of(begin + rows - 1)
    last_before = start_of(jnp.maximum(begin - 1, 0))
    span_begin = ctx_index * span
    last_span = start_of(span_begin + span - 1)
    to_end = (ts_count - 1 - ts_index).astype(jnp.float32)
    step_in = faded(1.0, last_own < begin)
    running, entered = state, jnp.zeros_like(state)
    rest = state * faded(to_end, last_span <= begin + rows - 1)
    for hop in range(ts_count - 1):
        got = lax.ppermute(running.astype(jnp.bfloat16), "ts", [(hop, hop + 1)])
        back_hop = ts_count - 1 - hop
        got_rest = lax.ppermute(rest.astype(jnp.bfloat16), "ts", [(back_hop, back_hop - 1)])
        got = got.astype(jnp.float32)
        entered = entered + got
        running = running + step_in * got
        rest = rest + got_rest.astype(jnp.float32)
    whole = rest + faded(to_end + 1.0, last_span < begin) * entered
    whole = whole.astype(jnp.bfloat16)
    for hop in range(1, reach + 1):
        if hop >= ctx_count:
            break
        got = lax.ppermute(whole, "ctx", [(i, i + hop) for i in range(ctx_count - hop)])
        distance = (ts_index + (hop - 1) * ts_count).astype(jnp.float32)
        alive = last_before <= span_begin - (hop - 1) * span - 1
        entered = entered + faded(distance, alive) * got.astype(jnp.float32)

    partial, query = pl.pallas_call(
        local_kernel,
        grid=(tiles,),
        in_specs=[smem, smem, tile(), tile(), edge(), taps_tile, wheel_tile,
                  block((1, TILE), lambda i: (0, i))],
        out_specs=[tile(), tile()],
        out_shape=[wide(jnp.float32), wide(jnp.float32)],
        scratch_shapes=[
            pltpu.VMEM((EDGE + rows, LANES), jnp.float32),
            pltpu.VMEM((2, rows, PER * LANES), jnp.bfloat16),
        ],
        cost_estimate=pl.CostEstimate(
            flops=2 * rows * rows * width * PER, bytes_accessed=rows * width * 12, transcendentals=0
        ),
        name="local",
    )(doc_lengths, begin_array, product, projected, edges, taps, own_rows, skip_gain[None])

    return pl.pallas_call(
        final_kernel,
        grid=(tiles,),
        in_specs=[smem, smem, tile(), wheel_tile, tile(), state_tile, tile(), tile()],
        out_specs=tile(),
        out_shape=wide(jnp.bfloat16),
        scratch_shapes=[pltpu.VMEM((2, rows, PER * LANES), jnp.bfloat16)],
        name="final",
    )(doc_lengths, begin_array, before, medium_rows, decay, entered, partial, query)


def solution(mesh):
    return jax.shard_map(
        per_device,
        mesh=mesh,
        in_specs=(P(("ctx", "ts"), None), P(), P(), P(), P(), P(), P()),
        out_specs=P(("ctx", "ts"), None),
        check_vma=False,
    )
```
